768 devices in a mesh: dp: 128 (over z_hi, y, x, core), tensor: 6 (over z_lo).
Axes of the slice: x: 4, y: 8, z: 12 (z_hi: 2, z_lo: 6; z = z_hi * 6 + z_lo), core: 2. Of those that a mesh axis runs over, the one named last changes fastest.
Arguments:
- queries: bfloat16 [192, 128, 6144], P(None, 'dp', 'tensor')
- keys_values: bfloat16 [192, 128, 2048], P('tensor', 'dp')
- lengths: int32 [128], replicated, may hold values from 48 to 192
- route: int32 [1], replicated, may hold values from 1 to 7
- cotangent: bfloat16 [192, 128, 6144], P(None, 'dp', 'tensor'), may hold values from -6 to 6
- advantage: int32 [192, 128], P(None, 'dp'), may hold values from -1024 to 1024
Outputs:
- query_grads: bfloat16 [192, 128, 6144], P(None, 'dp', 'tensor')
- kv_grads: bfloat16 [192, 128, 2048], P('tensor', 'dp')
The draws below stay inside these ranges and needn't reach their ends.
Inputs may be any that keep to these rules, and one draw needn't show every extreme that they name: route is one code for all micro-batches; a shard and its partner lie in the same aligned group of 8 shards.
All inputs are finite; a program needn't handle non-finite values.
Results may differ from the reference program's by a relative error of at most 0.038.
Values may be sent and summed in bfloat16 or wider, within the bound.
A program may use at most 32 MiB of HBM per device.

```python
import jax
import jax.numpy as jnp
from jax import lax

Q_HEADS = 48
KV_HEADS = 8
HEAD_DIM = 128
SLOT = 192
ROLLS = 1
QW = 6144
ROLLOUTS = 128
N_DP = 128
N_TENSOR = 6


def aligned_signs(key):
    flips = jax.random.bernoulli(key, 0.5, (ROLLOUTS, KV_HEADS * HEAD_DIM))
    return jnp.where(flips, 1.0, -1.0).astype(jnp.float32)


def draw_keys_values(key, part):
    signs = aligned_signs(key)
    key = jax.random.fold_in(key, 5)
    shape = (SLOT, ROLLOUTS, 2 * KV_HEADS * HEAD_DIM)
    field = jax.random.normal(key, shape, jnp.float32)
    width = KV_HEADS * HEAD_DIM
    turns = jnp.where(jnp.arange(width) % 2 == 0, 1.0, -1.0).astype(jnp.float32)
    field = field.at[0, :, :width].set(4.0 * signs)
    field = field.at[1, :, :width].set(signs * (3.96875 + 0.25 * turns[None, :]))
    return jnp.clip(field, -6.0, 6.0).astype(jnp.bfloat16)


def draw_queries(key, part):
    signs = aligned_signs(key)
    key = jax.random.fold_in(key, 9)
    field_key, noise_key = jax.random.split(key)
    shape = (SLOT, ROLLOUTS, Q_HEADS * HEAD_DIM)
    field = jax.random.normal(field_key, shape, jnp.float32)
    head_signs = jnp.tile(signs, (1, Q_HEADS // KV_HEADS))
    strength = jnp.array([3.5, 4.5, 5.5], jnp.float32)
    noise = 0.3 * jax.random.normal(noise_key, (3, ROLLOUTS, Q_HEADS * HEAD_DIM), jnp.float32)
    field = field.at[2:5].set(strength[:, None, None] * head_signs[None] + noise)
    return jnp.clip(field, -6.0, 6.0).astype(jnp.bfloat16)


def plant(result, stream_key, smallest, high):
    longest = result.shape.index(max(result.shape))
    spots = []
    for shift in (0, 1):
        where = [jax.random.randint(jax.random.fold_in(stream_key, axis), (), 0, length) for axis, length in enumerate(result.shape)]
        where[longest] = (where[longest] + shift) % result.shape[longest]
        spots.append(tuple(where))
    return result.at[spots[0]].set(smallest).at[spots[1]].set(high)


def level_of(own_key, dims, shards, least, largest):
    factor_of, own = 1.0, jax.random.fold_in(own_key, 6)
    for axis_at, parts in shards:
        steps = jnp.exp(jax.random.uniform(jax.random.fold_in(own, axis_at), (parts,), jnp.float32, least / len(shards), largest / len(shards)))
        factor_of = factor_of * jnp.repeat(steps, dims[axis_at] // parts).reshape([-1 if axis == axis_at else 1 for axis in range(len(dims))])
    return factor_of


def normal_values(rng, extent, scale, bound, cuts=(), kind=jnp.bfloat16):
    result = scale * jax.random.normal(rng, extent, jnp.float32)
    if cuts:
        result = result * level_of(rng, extent, cuts, -0.22, 0.18)
    return jnp.clip(result, -bound, bound).astype(kind)


def setup_inputs(seed: int = 0) -> dict:
    arg_keys = jax.random.split(jax.random.key(seed), 7)
    return {
        "queries": draw_queries(jax.random.fold_in(arg_keys[6], 71), 0),
        "keys_values": draw_keys_values(jax.random.fold_in(arg_keys[6], 71), 0),
        "lengths": plant(jax.random.randint(arg_keys[2], (ROLLOUTS,), SLOT // 4, SLOT + 1), jax.random.fold_in(arg_keys[2], 1), SLOT // 4, SLOT).astype(jnp.int32),
        "route": jax.random.randint(arg_keys[3], (1,), 1, 8).astype(jnp.int32),
        "cotangent": normal_values(arg_keys[4], (SLOT, ROLLOUTS, QW), 1.0, 6.0, ((1, 128), (2, 6))),
        "advantage": plant(jax.random.randint(arg_keys[5], (SLOT, ROLLOUTS), -1024, 1025), jax.random.fold_in(arg_keys[5], 1), -1024, 1024).astype(jnp.int32),
    }


def one_rollout(query, keyval, grad, length):
    slot = query.shape[0]
    kvw = keyval.shape[1] // 2
    kvh = kvw // HEAD_DIM
    groups = query.shape[1] // kvw
    blocks = N_TENSOR
    per_block = groups // blocks
    scale = 1.0 / (HEAD_DIM ** 0.5)
    qh = query.astype(jnp.float32).reshape(slot, groups, kvh, HEAD_DIM)
    kh = keyval[:, :kvw].astype(jnp.float32).reshape(slot, kvh, HEAD_DIM)
    vh = keyval[:, kvw:].astype(jnp.float32).reshape(slot, kvh, HEAD_DIM)
    gh = grad.astype(jnp.float32).reshape(slot, groups, kvh, HEAD_DIM)
    scores = jnp.einsum('pgkd,qkd->gkpq', qh, kh) * scale
    place = jnp.arange(slot)
    allowed = (place[None, :] <= place[:, None]) & (place[None, :] < length)
    scores = jnp.where(allowed[None, None], scores, -1e30)
    top = jnp.max(scores, axis=-1, keepdims=True)
    expo = jnp.exp(scores - top)
    probs = expo / jnp.sum(expo, axis=-1, keepdims=True)
    probs_b = lax.optimization_barrier(probs.astype(jnp.bfloat16)).astype(jnp.float32)
    attn = jnp.einsum('gkpq,qkd->pgkd', probs_b, vh)
    delta = jnp.sum(gh * attn, axis=-1)
    dprob = jnp.einsum('pgkd,qkd->gkpq', gh, vh)
    dscore = probs * (dprob - jnp.transpose(delta, (1, 2, 0))[..., None])
    dscore = lax.optimization_barrier(dscore.astype(jnp.bfloat16)).astype(jnp.float32)
    dquery = (jnp.einsum('gkpq,qkd->pgkd', dscore, kh) * scale).astype(jnp.bfloat16).reshape(slot, -1)
    ds_blocks = dscore.reshape(blocks, per_block, kvh, slot, slot)
    pb_blocks = probs_b.reshape(blocks, per_block, kvh, slot, slot)
    q_blocks = qh.reshape(slot, blocks, per_block, kvh, HEAD_DIM)
    g_blocks = gh.reshape(slot, blocks, per_block, kvh, HEAD_DIM)
    dkey = jnp.einsum('tgkpq,ptgkd->tqkd', ds_blocks, q_blocks) * scale
    dval = jnp.einsum('tgkpq,ptgkd->tqkd', pb_blocks, g_blocks)
    part = jnp.concatenate([dkey.reshape(blocks, slot, kvw), dval.reshape(blocks, slot, kvw)], axis=-1)
    part = lax.optimization_barrier(part.astype(jnp.bfloat16)).astype(jnp.float32)
    dkv = jnp.sum(part, axis=0).astype(jnp.bfloat16)
    return dquery, dkv


def reference(queries, keys_values, lengths, route, cotangent, advantage):
    index = jnp.arange(ROLLOUTS, dtype=jnp.int32)
    shard = index // ROLLS
    member = index % ROLLS
    dest = jnp.where(member == 0, (jnp.bitwise_xor(shard, route[0]) * ROLLS).astype(jnp.int32), index).astype(jnp.int32)
    slot_len = lengths[dest]
    count = jnp.sum(slot_len.reshape(N_DP, ROLLS), axis=1).astype(jnp.float32)
    factor = (ROLLS * SLOT) / count
    place = jnp.arange(SLOT)
    live = (place[:, None] < slot_len[None, :]).astype(jnp.float32)
    weight = (advantage.astype(jnp.float32) / 256.0 * factor[shard][None, :]) * live

    def each_rollout(rollout):
        moved = dest[rollout]
        cot_column = lax.dynamic_index_in_dim(cotangent, moved, 1, keepdims=False)
        weight_column = lax.dynamic_index_in_dim(weight, moved, 1, keepdims=False)
        grad = (cot_column.astype(jnp.float32) * weight_column[:, None]).astype(jnp.bfloat16)
        query = lax.dynamic_index_in_dim(queries, rollout, 1, keepdims=False)
        keyval = lax.dynamic_index_in_dim(keys_values, rollout, 1, keepdims=False)
        return one_rollout(query, keyval, grad, lengths[rollout])

    dquery, dkv = lax.map(each_rollout, index)
    return jnp.moveaxis(dquery, 0, 1), jnp.moveaxis(dkv, 0, 1)
```

```python
import functools

import jax
import jax.numpy as jnp
from jax import lax
from jax.experimental import pallas as pl
from jax.experimental.pallas import tpu as pltpu
from jax.sharding import PartitionSpec as P

HEAD_DIM = 128
MESH = pl.DeviceIdType.MESH
NT = (((1,), (1,)), ((), ()))
NN = (((1,), (0,)), ((), ()))
TN = (((0,), (0,)), ((), ()))


def dot(a, b, dims):
    return lax.dot_general(a, b, dims, preferred_element_type=jnp.float32)


def kernel(
    nt, nh,
    len_ref, route_ref, adv_ref, q_hbm, kv_hbm, cot_hbm, dq_hbm, dkv_hbm,
    q, cot, kvin, kvb, g0, gsib, sel1, ga, sela, gb, part, upb, dnb, dqb, dkvb,
    in_sem, dq_sem, dkv_sem,
    kv_r, kv_su, kv_sd, ru_r, ru_s, rd_r, rd_s,
    sib_s, sib_r, a_s, a_r, b_s, b_r,
):
    dp = lax.axis_index("dp")
    t = lax.axis_index("tensor")
    slot = q.shape[0]
    rows = slot // nt
    kvw = nh * HEAD_DIM
    last = nt - 1
    core = lax.rem(dp, 2)
    x = lax.rem(lax.div(dp, 2), 4)
    sib = dp + 1 - 2 * core
    near_a = dp + 2 * (1 - 2 * lax.rem(x, 2))
    near_b = dp + 2 * (3 - 2 * x)
    up = jnp.minimum(t + 1, last)
    down = jnp.maximum(t - 1, 0)
    scale = 1.0 / HEAD_DIM**0.5

    load_kv = pltpu.make_async_copy(kv_hbm, kvin, in_sem.at[0])
    load_cot = pltpu.make_async_copy(cot_hbm, cot, in_sem.at[1])
    load_q = pltpu.make_async_copy(q_hbm, q, in_sem.at[2])
    load_kv.start()
    load_cot.start()
    load_q.start()

    barrier = pltpu.get_barrier_semaphore()

    def greet(where, index):
        pl.semaphore_signal(barrier, inc=1, device_id=(where, index), device_id_type=MESH)

    greet(sib, t)
    greet(near_a, t)
    greet(near_b, t)

    @pl.when(t < last)
    def _():
        greet(dp, up)

    @pl.when(t > 0)
    def _():
        greet(dp, down)

    def remote(src, dst, send, recv, where, index):
        return pltpu.make_async_remote_copy(
            src_ref=src, dst_ref=dst, send_sem=send, recv_sem=recv, device_id=(where, index), device_id_type=MESH
        )

    def band(s):
        return pl.ds(pl.multiple_of(s * rows, rows), rows)

    def kv_up(s, h):
        block = kvb.at[h, band(s)]
        return remote(block, block, kv_su.at[s, h], kv_r.at[s, h], dp, up)

    def kv_down(s, h):
        block = kvb.at[h, band(s)]
        return remote(block, block, kv_sd.at[s, h], kv_r.at[s, h], dp, down)

    def sum_up(src, s, h):
        return remote(src.at[h, band(s)], upb.at[h, band(s)], ru_s.at[s, h], ru_r.at[s, h], dp, up)

    def sum_down(src, s, h):
        return remote(src.at[h, band(s)], dnb.at[h, band(s)], rd_s.at[s, h], rd_r.at[s, h], dp, down)

    def to_sib(h):
        return remote(g0.at[h], gsib.at[h], sib_s.at[h], sib_r.at[h], sib, t)

    def to_a(h):
        return remote(sel1.at[h], ga.at[h], a_s.at[h], a_r.at[h], near_a, t)

    def to_b(h):
        return remote(sela.at[h], gb.at[h], b_s.at[h], b_r.at[h], near_b, t)

    def head(h):
        return pl.ds(pl.multiple_of(h * HEAD_DIM, HEAD_DIM), HEAD_DIM)

    def value_head(h):
        return pl.ds(pl.multiple_of(kvw + h * HEAD_DIM, HEAD_DIM), HEAD_DIM)

    load_kv.wait()

    @pl.loop(0, nh)
    def _(h):
        kvb[h, band(t), 0:HEAD_DIM] = kvin[:, head(h)]
        kvb[h, band(t), HEAD_DIM : 2 * HEAD_DIM] = kvin[:, value_head(h)]

    pl.semaphore_wait(barrier, 3 + (t > 0).astype(jnp.int32) + (t < last).astype(jnp.int32))

    @pl.loop(0, nh)
    def _(h):
        @pl.when(t < last)
        def _():
            kv_up(t, h).start()

        @pl.when(t > 0)
        def _():
            kv_down(t, h).start()

    code = route_ref[0]
    moved = jnp.bitwise_xor(dp, code)
    slot_len = len_ref[moved]
    factor = slot / jnp.full((1, slot), slot_len, jnp.int32).astype(jnp.float32)
    place = lax.broadcasted_iota(jnp.int32, (1, slot), 1)
    live = (place < slot_len).astype(jnp.float32)
    weight = adv_ref[...].astype(jnp.float32) / 256.0 * factor * live
    weight = jnp.broadcast_to(weight, (HEAD_DIM, slot)).T
    load_cot.wait()

    @pl.loop(0, nh)
    def _(h):
        g0[h] = (cot[:, head(h)].astype(jnp.float32) * weight).astype(jnp.bfloat16)
        to_sib(h).start()

    x_code = jnp.bitwise_and(lax.shift_right_logical(code, 1), 3)
    use_sib = jnp.full((1, HEAD_DIM), jnp.bitwise_and(code, 1), jnp.int32) == 1
    x_full = jnp.full((1, HEAD_DIM), x_code, jnp.int32)
    use_a = jnp.logical_or(x_full == 1, x_full == 2)
    use_b = x_full >= 2

    @pl.loop(0, nh)
    def _(h):
        to_sib(h).wait_recv()
        sel1[h] = jnp.where(use_sib, gsib[h], g0[h])
        to_a(h).start()

    def hop_b(h):
        to_a(h).wait_recv()
        sela[h] = jnp.where(use_a, ga[h], sel1[h])
        to_b(h).start()

    def gather(h):
        for d in range(1, nt):
            s_lo = t - d
            s_hi = t + d

            @pl.when(s_lo >= 0)
            def _():
                kv_up(s_lo, h).wait_recv()

                @pl.when(t < last)
                def _():
                    kv_up(s_lo, h).start()

            @pl.when(s_hi <= last)
            def _():
                kv_down(s_hi, h).wait_recv()

                @pl.when(t > 0)
                def _():
                    kv_down(s_hi, h).start()

    home_len = len_ref[dp]
    key_at = lax.broadcasted_iota(jnp.int32, (slot, slot), 0)
    query_at = lax.broadcasted_iota(jnp.int32, (slot, slot), 1)

    def compute(h):
        to_b(h).wait_recv()
        grad = jnp.where(use_b, gb[h], sela[h])
        query = q[:, head(h)]
        key = kvb[h, :, 0:HEAD_DIM]
        value = kvb[h, :, HEAD_DIM : 2 * HEAD_DIM]
        allowed = jnp.logical_and(key_at <= query_at, key_at < home_len)
        scores = dot(key, query, NT) * scale
        dprob = dot(value, grad, NT)
        scores = jnp.where(allowed, scores, -1e30)
        expo = jnp.exp(scores - jnp.max(scores, axis=0, keepdims=True))
        probs = expo * (1.0 / jnp.sum(expo, axis=0, keepdims=True))
        probs_b = probs.astype(jnp.bfloat16)
        delta = jnp.sum(probs_b.astype(jnp.float32) * dprob, axis=0, keepdims=True)
        dscore = (probs * (dprob - delta)).astype(jnp.bfloat16)
        part[h, :, 0:HEAD_DIM] = (dot(dscore, query, NN) * scale).astype(jnp.bfloat16)
        part[h, :, HEAD_DIM : 2 * HEAD_DIM] = dot(probs_b, grad, NN).astype(jnp.bfloat16)

        @pl.when(t == 0)
        def _():
            for s in range(last, 0, -1):
                sum_up(part, s, h).start()

        @pl.when(t == last)
        def _():
            for s in range(last):
                sum_down(part, s, h).start()

        dqb[:, head(h)] = (dot(dscore, key, TN) * scale).astype(jnp.bfloat16)
        store_dq(h).start()

    def store_dq(h):
        return pltpu.make_async_copy(dqb.at[:, head(h)], dq_hbm.at[:, head(h)], dq_sem.at[h])

    def add(buf, s, h):
        total = buf[h, band(s)].astype(jnp.float32) + part[h, band(s)].astype(jnp.float32)
        buf[h, band(s)] = total.astype(jnp.bfloat16)

    def relay_up(h):
        for s in range(last, 1, -1):

            @pl.when(t < s)
            def _():
                sum_up(upb, s, h).wait_recv()
                add(upb, s, h)
                sum_up(upb, s, h).start()

    def relay_down(h):
        for s in range(last - 1):

            @pl.when(t > s)
            def _():
                sum_down(dnb, s, h).wait_recv()
                add(dnb, s, h)
                sum_down(dnb, s, h).start()

    def finish(h):
        @pl.when(t > 0)
        def _():
            sum_up(upb, t, h).wait_recv()

        @pl.when(t < last)
        def _():
            sum_down(dnb, t, h).wait_recv()

        has_up = jnp.full((1, 2 * HEAD_DIM), t, jnp.int32) > 0
        has_down = jnp.full((1, 2 * HEAD_DIM), t, jnp.int32) < last
        total = part[h, band(t)].astype(jnp.float32)
        total += jnp.where(has_up, upb[h, band(t)].astype(jnp.float32), 0.0)
        total += jnp.where(has_down, dnb[h, band(t)].astype(jnp.float32), 0.0)
        total = total.astype(jnp.bfloat16)
        dkvb[:, head(h)] = total[:, 0:HEAD_DIM]
        dkvb[:, value_head(h)] = total[:, HEAD_DIM:]

    hop_b(0)
    load_q.wait()

    @pl.loop(0, nh + last)
    def _(n):
        @pl.when(n + 1 < nh)
        def _():
            hop_b(n + 1)

        @pl.when(n < nh)
        def _():
            gather(n)
            compute(n)

        h_up = n - t
        h_down = n - (last - t)

        @pl.when(jnp.logical_and(t > 0, jnp.logical_and(h_up >= 0, h_up < nh)))
        def _():
            relay_up(h_up)

        @pl.when(jnp.logical_and(t < last, jnp.logical_and(h_down >= 0, h_down < nh)))
        def _():
            relay_down(h_down)

        @pl.when(n >= last)
        def _():
            finish(n - last)

    store_dkv = pltpu.make_async_copy(dkvb, dkv_hbm, dkv_sem)
    store_dkv.start()

    @pl.loop(0, nh)
    def _(h):
        to_sib(h).wait_send()
        to_a(h).wait_send()
        to_b(h).wait_send()
        store_dq(h).wait()
        for s in range(nt):

            @pl.when(jnp.logical_and(t < last, s <= t))
            def _():
                kv_up(s, h).wait_send()

            @pl.when(jnp.logical_and(t > 0, s >= t))
            def _():
                kv_down(s, h).wait_send()

            @pl.when(s > t)
            def _():
                sum_up(upb, s, h).wait_send()

            @pl.when(s < t)
            def _():
                sum_down(dnb, s, h).wait_send()

    store_dkv.wait()


def on_device(queries, keys_values, lengths, route, cotangent, advantage):
    slot, _, qwidth = queries.shape
    rows, _, kv2 = keys_values.shape
    nt = lax.axis_size("tensor")
    nh = kv2 // 2 // HEAD_DIM
    wide = 2 * HEAD_DIM
    bf16 = jnp.bfloat16
    heads = pltpu.VMEM((nh, slot, HEAD_DIM), bf16)
    blocks = pltpu.VMEM((nh, slot, wide), bf16)
    dma = pltpu.SemaphoreType.DMA
    dq, dkv = pl.pallas_call(
        functools.partial(kernel, nt, nh),
        out_shape=(
            jax.ShapeDtypeStruct((slot, qwidth), bf16),
            jax.ShapeDtypeStruct((rows, kv2), bf16),
        ),
        in_specs=[
            pl.BlockSpec(memory_space=pltpu.SMEM),
            pl.BlockSpec(memory_space=pltpu.SMEM),
            pl.BlockSpec(memory_space=pltpu.VMEM),
            pl.BlockSpec(memory_space=pl.ANY),
            pl.BlockSpec(memory_space=pl.ANY),
            pl.BlockSpec(memory_space=pl.ANY),
        ],
        out_specs=(pl.BlockSpec(memory_space=pl.ANY), pl.BlockSpec(memory_space=pl.ANY)),
        scratch_shapes=[
            pltpu.VMEM((slot, qwidth), bf16),
            pltpu.VMEM((slot, qwidth), bf16),
            pltpu.VMEM((rows, kv2), bf16),
            blocks,
            heads, heads, heads, heads, heads, heads,
            blocks, blocks, blocks,
            pltpu.VMEM((slot, qwidth), bf16),
            pltpu.VMEM((rows, kv2), bf16),
            dma((3,)), dma((nh,)), dma,
            dma((nt, nh)), dma((nt, nh)), dma((nt, nh)),
            dma((nt, nh)), dma((nt, nh)), dma((nt, nh)), dma((nt, nh)),
            dma((nh,)), dma((nh,)), dma((nh,)), dma((nh,)), dma((nh,)), dma((nh,)),
        ],
        compiler_params=pltpu.CompilerParams(
            collective_id=0, has_side_effects=True, vmem_limit_bytes=60 * 1024 * 1024
        ),
        name="attention_grads",
    )(
        lengths,
        route,
        advantage.reshape(1, slot),
        queries.reshape(slot, qwidth),
        keys_values.reshape(rows, kv2),
        cotangent.reshape(slot, qwidth),
    )
    return dq.reshape(slot, 1, qwidth), dkv.reshape(rows, 1, kv2)


def solution(mesh):
    placed = (
        P(None, "dp", "tensor"),
        P("tensor", "dp", None),
        P(),
        P(),
        P(None, "dp", "tensor"),
        P(None, "dp"),
    )
    return jax.shard_map(
        on_device,
        mesh=mesh,
        in_specs=placed,
        out_specs=(P(None, "dp", "tensor"), P("tensor", "dp", None)),
        check_vma=False,
    )
```

```python
import functools

import jax
import jax.numpy as jnp
from jax import lax
from jax.experimental import pallas as pl
from jax.experimental.pallas import tpu as pltpu
from jax.sharding import PartitionSpec as P

HEAD_DIM = 128
MESH = pl.DeviceIdType.MESH
NT = (((1,), (1,)), ((), ()))
NN = (((1,), (0,)), ((), ()))
TN = (((0,), (0,)), ((), ()))


def dot(a, b, dims):
    return lax.dot_general(a, b, dims, preferred_element_type=jnp.float32)


LINE = 6
HEADS = (1, 2, 2, 2, 1)
AHEAD = 1
ISSUED = 2
RELAY_LAG = 1
FINISH_LAG = 2

TWO_STOPS = ((0, 1, 0, 3, 3), (1, 2, 1, 4), (2, 2, 4), (3, 4), (4,))
KV_TREES = (TWO_STOPS,) * len(HEADS)
SUM_TREES = (TWO_STOPS,) * len(HEADS)


def plan(tree):
    copies = []
    for s, parents in enumerate(tree):
        for i, a in enumerate(parents):
            b = s + 1 + i
            copies.append((s, a, b))
            copies.append((LINE - 1 - s, LINE - 1 - a, LINE - 1 - b))
    copies.sort(key=lambda c: (abs(c[0] - c[1]), -abs(c[0] - c[2]), c))
    used = [0] * LINE
    edges = []
    for s, a, b in copies:
        edges.append((s, a, b, used[a]))
        used[a] += 1
    return edges


def outgoing(edges, s, a):
    return [e for e in edges if e[0] == s and e[1] == a]


def stops(edges):
    return sorted({(s, a) for s, a, _, _ in edges if s != a}, key=lambda c: (abs(c[0] - c[1]), c))


STEPS = len(HEADS)
FIRST = [sum(HEADS[:n]) for n in range(STEPS)]
KV_EDGES = [plan(tree) for tree in KV_TREES]
SUM_EDGES = [plan(tree) for tree in SUM_TREES]
KV_SLOTS = 1 + max(e[3] for edges in KV_EDGES for e in edges)
SUM_SLOTS = [1 + max(e[3] for e in edges) for edges in SUM_EDGES]
PARTNERS = {frozenset((e[1], e[2])) for edges in KV_EDGES + SUM_EDGES for e in edges}


def one_of(t, members):
    found = t == members[0]
    for m in members[1:]:
        found = jnp.logical_or(found, t == m)
    return found


def kernel(nt, nh, len_ref, route_ref, adv_ref, q_hbm, kv_hbm, cot_hbm, dq_hbm, dkv_hbm, *scratch):
    scratch = list(scratch)

    def take(count):
        taken = scratch[:count]
        del scratch[:count]
        return taken

    q, cot, dqb, dkvb = take(4)
    kvb, part, sums, arrived = take(STEPS), take(STEPS), take(STEPS), take(STEPS)
    g0, gsib, sel1, ga, sela, gb = [take(STEPS) for _ in range(6)]
    in_sem, own_sem, dq_sem, dkv_sem = take(4)
    kv_r, kv_s, sum_r, sum_s = take(4)
    sib_s, sib_r, a_s, a_r, b_s, b_r = take(6)

    dp = lax.axis_index("dp")
    t = lax.axis_index("tensor")
    slot = q.shape[0]
    rows = slot // nt
    kvw = nh * HEAD_DIM
    core = lax.rem(dp, 2)
    x = lax.rem(lax.div(dp, 2), 4)
    sib = dp + 1 - 2 * core
    near_a = dp + 2 * (1 - 2 * lax.rem(x, 2))
    near_b = dp + 2 * (3 - 2 * x)
    scale = 1.0 / HEAD_DIM**0.5

    barrier = pltpu.get_barrier_semaphore()

    def greet(where, index):
        pl.semaphore_signal(barrier, inc=1, device_id=(where, index), device_id_type=MESH)

    greet(sib, t)
    greet(near_a, t)
    greet(near_b, t)
    greetings = 3
    for s in range(nt):
        met = [m for m in range(nt) if frozenset((m, s)) in PARTNERS]

        @pl.when(one_of(t, met))
        def _():
            greet(dp, s)

        greetings += one_of(t, met).astype(jnp.int32)

    def remote(src, dst, send, recv, where, index):
        return pltpu.make_async_remote_copy(
            src_ref=src, dst_ref=dst, send_sem=send, recv_sem=recv, device_id=(where, index), device_id_type=MESH
        )

    def band(s):
        return pl.ds(pl.multiple_of(s * rows, rows), rows)

    def columns(n, start=0):
        return pl.ds(start + FIRST[n] * HEAD_DIM, HEADS[n] * HEAD_DIM)

    def halves(n):
        group = HEADS[n] * HEAD_DIM
        return ((columns(n), pl.ds(0, group)), (columns(n, kvw), pl.ds(group, group)))

    def own(n):
        block = kvb[n].at[band(t)]
        return pltpu.make_async_copy(block, block, own_sem.at[n])

    def kv_copy(edge, n):
        s, _, b, k = edge
        block = kvb[n].at[band(s)]
        return remote(block, block, kv_s.at[k, n], kv_r.at[s, n], dp, b)

    def kv_arrival(s, n):
        block = kvb[n].at[band(s)]
        return remote(block, block, kv_s.at[0, n], kv_r.at[s, n], dp, t)

    def sum_copy(src, edge, n):
        s, a, _, k = edge
        return remote(src[n].at[band(s)], arrived[n].at[k], sum_s.at[s, n], sum_r.at[k, n], dp, a)

    def to_sib(n):
        return remote(g0[n], gsib[n], sib_s.at[n], sib_r.at[n], sib, t)

    def to_a(n):
        return remote(sel1[n], ga[n], a_s.at[n], a_r.at[n], near_a, t)

    def to_b(n):
        return remote(sela[n], gb[n], b_s.at[n], b_r.at[n], near_b, t)

    def load_own(n):
        for there, here in halves(n):
            pltpu.make_async_copy(kv_hbm.at[:, there], kvb[n].at[band(t), here], own_sem.at[n]).start()

    def direct(n):
        for edge in KV_EDGES[n]:
            s, a, b, k = edge
            if s == a:

                @pl.when(t == a)
                def _():
                    for there, here in halves(n):
                        remote(
                            kv_hbm.at[:, there], kvb[n].at[band(s), here], kv_s.at[k, n], kv_r.at[s, n], dp, b
                        ).start()

    def relay(n):
        for s, a in stops(KV_EDGES[n]):

            @pl.when(t == a)
            def _():
                kv_arrival(s, n).wait_recv()
                for edge in outgoing(KV_EDGES[n], s, a):
                    kv_copy(edge, n).start()

    def arrive(n):
        own(n).wait()
        for s in range(nt):
            leaves = [m for m in range(nt) if m != s and not outgoing(KV_EDGES[n], s, m)]

            @pl.when(one_of(t, leaves))
            def _():
                kv_arrival(s, n).wait_recv()

    load_cot = pltpu.make_async_copy(cot_hbm, cot, in_sem.at[0])
    load_q = pltpu.make_async_copy(q_hbm, q, in_sem.at[1])
    load_cot.start()
    pl.semaphore_wait(barrier, greetings)
    for n in range(min(ISSUED, STEPS)):
        direct(n)
    for n in range(STEPS):
        load_own(n)
    load_q.start()

    code = route_ref[0]
    moved = jnp.bitwise_xor(dp, code)
    slot_len = len_ref[moved]
    factor = slot / jnp.full((1, slot), slot_len, jnp.int32).astype(jnp.float32)
    place = lax.broadcasted_iota(jnp.int32, (1, slot), 1)
    live = (place < slot_len).astype(jnp.float32)
    weight = adv_ref[...].astype(jnp.float32) / 256.0 * factor * live
    weight = jnp.broadcast_to(weight, (HEAD_DIM, slot)).T
    load_cot.wait()
    for n in range(STEPS):
        wide = jnp.concatenate([weight] * HEADS[n], axis=1)
        g0[n][...] = (cot[:, columns(n)].astype(jnp.float32) * wide).astype(jnp.bfloat16)
        to_sib(n).start()

    x_code = jnp.bitwise_and(lax.shift_right_logical(code, 1), 3)

    def chosen(n, flag):
        return jnp.full((1, HEADS[n] * HEAD_DIM), flag, jnp.int32) == 1

    use_sib = jnp.bitwise_and(code, 1)
    use_a = jnp.logical_or(x_code == 1, x_code == 2).astype(jnp.int32)
    use_b = (x_code >= 2).astype(jnp.int32)

    for n in range(STEPS):
        to_sib(n).wait_recv()
        sel1[n][...] = jnp.where(chosen(n, use_sib), gsib[n][...], g0[n][...])
        to_a(n).start()

    def hop_b(n):
        to_a(n).wait_recv()
        sela[n][...] = jnp.where(chosen(n, use_a), ga[n][...], sel1[n][...])
        to_b(n).start()

    home_len = len_ref[dp]
    key_at = lax.broadcasted_iota(jnp.int32, (slot, slot), 0)
    query_at = lax.broadcasted_iota(jnp.int32, (slot, slot), 1)

    def one_head(n, j, grad):
        here = pl.ds(j * HEAD_DIM, HEAD_DIM)
        there = pl.ds((HEADS[n] + j) * HEAD_DIM, HEAD_DIM)
        at = pl.ds((FIRST[n] + j) * HEAD_DIM, HEAD_DIM)
        query = q[:, at]
        key = kvb[n][:, here]
        value = kvb[n][:, there]
        allowed = jnp.logical_and(key_at <= query_at, key_at < home_len)
        scores = dot(key, query, NT) * scale
        dprob = dot(value, grad, NT)
        scores = jnp.where(allowed, scores, -1e30)
        expo = jnp.exp(scores - jnp.max(scores, axis=0, keepdims=True))
        probs = expo * (1.0 / jnp.sum(expo, axis=0, keepdims=True))
        probs_b = probs.astype(jnp.bfloat16)
        delta = jnp.sum(probs_b.astype(jnp.float32) * dprob, axis=0, keepdims=True)
        dscore = (probs * (dprob - delta)).astype(jnp.bfloat16)
        part[n][:, here] = (dot(dscore, query, NN) * scale).astype(jnp.bfloat16)
        part[n][:, there] = dot(probs_b, grad, NN).astype(jnp.bfloat16)
        dqb[:, at] = (dot(dscore, key, TN) * scale).astype(jnp.bfloat16)

    def compute(n):
        to_b(n).wait_recv()
        grad = jnp.where(chosen(n, use_b), gb[n][...], sela[n][...])
        for j in range(HEADS[n]):
            one_head(n, j, grad[:, j * HEAD_DIM : (j + 1) * HEAD_DIM])
        for edge in SUM_EDGES[n]:
            if not outgoing(SUM_EDGES[n], edge[0], edge[2]):

                @pl.when(t == edge[2])
                def _():
                    sum_copy(part, edge, n).start()

        store_dq(n).start()

    def store_dq(n):
        return pltpu.make_async_copy(dqb.at[:, columns(n)], dq_hbm.at[:, columns(n)], dq_sem.at[n])

    def collect(s, a, n):
        total = part[n][band(s)].astype(jnp.float32)
        for edge in outgoing(SUM_EDGES[n], s, a):
            sum_copy(sums, edge, n).wait_recv()
            total += arrived[n][edge[3]].astype(jnp.float32)
        return total.astype(jnp.bfloat16)

    def relay_sums(n):
        for s, a in reversed(stops(SUM_EDGES[n])):
            into = [e for e in SUM_EDGES[n] if e[0] == s and e[2] == a][0]

            @pl.when(t == a)
            def _():
                sums[n][band(s)] = collect(s, a, n)
                sum_copy(sums, into, n).start()

    def store_dkv(n, half):
        there = halves(n)[half][0]
        return pltpu.make_async_copy(dkvb.at[:, there], dkv_hbm.at[:, there], dkv_sem.at[n, half])

    def finish(n):
        group = HEADS[n] * HEAD_DIM
        for s in range(nt):

            @pl.when(t == s)
            def _():
                total = collect(s, s, n)
                dkvb[:, columns(n)] = total[:, 0:group]
                dkvb[:, columns(n, kvw)] = total[:, group:]

        store_dkv(n, 0).start()
        store_dkv(n, 1).start()

    def sums_sent(n):
        for edge in SUM_EDGES[n]:

            @pl.when(t == edge[2])
            def _():
                sum_copy(sums, edge, n).wait_send()

    def sent(n):
        to_sib(n).wait_send()
        to_a(n).wait_send()
        to_b(n).wait_send()
        store_dq(n).wait()
        for edge in KV_EDGES[n]:

            @pl.when(t == edge[1])
            def _():
                kv_copy(edge, n).wait_send()

    for n in range(AHEAD):
        relay(n)
    hop_b(0)
    load_q.wait()

    for n in range(STEPS + FINISH_LAG):
        if n + ISSUED < STEPS:
            direct(n + ISSUED)
        if n + AHEAD < STEPS:
            relay(n + AHEAD)
        if n + 1 < STEPS:
            hop_b(n + 1)
        if n < STEPS:
            arrive(n)
            compute(n)
        if RELAY_LAG <= n < STEPS + RELAY_LAG:
            relay_sums(n - RELAY_LAG)
        if n == STEPS + RELAY_LAG - 1:
            for m in range(STEPS):
                sent(m)
            for m in range(STEPS - 1):
                sums_sent(m)
        if n >= FINISH_LAG:
            finish(n - FINISH_LAG)

    sums_sent(STEPS - 1)
    for n in range(STEPS):
        store_dkv(n, 0).wait()
        store_dkv(n, 1).wait()


def on_device(queries, keys_values, lengths, route, cotangent, advantage):
    slot, _, qwidth = queries.shape
    rows, _, kv2 = keys_values.shape
    nt = lax.axis_size("tensor")
    nh = kv2 // 2 // HEAD_DIM
    bf16 = jnp.bfloat16
    dma = pltpu.SemaphoreType.DMA
    smem = pl.BlockSpec(memory_space=pltpu.SMEM)
    hbm = pl.BlockSpec(memory_space=pl.ANY)
    width = [h * HEAD_DIM for h in HEADS]
    blocks = [pltpu.VMEM((slot, 2 * w), bf16) for w in width]
    grads = [pltpu.VMEM((slot, w), bf16) for w in width]
    dq, dkv = pl.pallas_call(
        functools.partial(kernel, nt, nh),
        out_shape=(
            jax.ShapeDtypeStruct((slot, qwidth), bf16),
            jax.ShapeDtypeStruct((rows, kv2), bf16),
        ),
        in_specs=[smem, smem, pl.BlockSpec(memory_space=pltpu.VMEM), hbm, hbm, hbm],
        out_specs=(hbm, hbm),
        scratch_shapes=[
            pltpu.VMEM((slot, qwidth), bf16),
            pltpu.VMEM((slot, qwidth), bf16),
            pltpu.VMEM((slot, qwidth), bf16),
            pltpu.VMEM((rows, kv2), bf16),
            *blocks, *blocks, *blocks,
            *[pltpu.VMEM((k, rows, 2 * w), bf16) for k, w in zip(SUM_SLOTS, width)],
            *(grads * 6),
            dma((2,)), dma((STEPS,)), dma((STEPS,)), dma((STEPS, 2)),
            dma((nt, STEPS)), dma((KV_SLOTS, STEPS)), dma((max(SUM_SLOTS), STEPS)), dma((nt, STEPS)),
            *([dma((STEPS,))] * 6),
        ],
        compiler_params=pltpu.CompilerParams(
            collective_id=0, has_side_effects=True, vmem_limit_bytes=60 * 1024 * 1024
        ),
        name="attention_grads",
    )(
        lengths,
        route,
        advantage.reshape(1, slot),
        queries.reshape(slot, qwidth),
        keys_values.reshape(rows, kv2),
        cotangent.reshape(slot, qwidth),
    )
    return dq.reshape(slot, 1, qwidth), dkv.reshape(rows, 1, kv2)


def solution(mesh):
    placed = (
        P(None, "dp", "tensor"),
        P("tensor", "dp", None),
        P(),
        P(),
        P(None, "dp", "tensor"),
        P(None, "dp"),
    )
    return jax.shard_map(
        on_device,
        mesh=mesh,
        in_specs=placed,
        out_specs=(P(None, "dp", "tensor"), P("tensor", "dp", None)),
        check_vma=False,
    )
```

```python
import functools

import jax
import jax.numpy as jnp
from jax import lax
from jax.experimental import pallas as pl
from jax.experimental.pallas import tpu as pltpu
from jax.sharding import PartitionSpec as P

HEAD_DIM = 128
MESH = pl.DeviceIdType.MESH
NT = (((1,), (1,)), ((), ()))
NN = (((1,), (0,)), ((), ()))
TN = (((0,), (0,)), ((), ()))


def dot(a, b, dims):
    return lax.dot_general(a, b, dims, preferred_element_type=jnp.float32)


LINE = 6
HEADS = (2, 2, 2, 2)
AHEAD = 2
ISSUED = 4
RELAY_LAG = 2
FINISH_LAG = 4

TWO_STOPS = ((0, 1, 0, 3, 3), (1, 2, 1, 4), (2, 2, 4), (3, 4), (4,))
KV_TREES = ((TWO_STOPS, TWO_STOPS),) * len(HEADS)
SUM_TREES = ((TWO_STOPS, TWO_STOPS),) * len(HEADS)


def plan(trees, key):
    above, below = trees
    copies = []
    for s, parents in enumerate(above):
        copies += [(s, a, s + 1 + i) for i, a in enumerate(parents)]
    for s, parents in enumerate(below):
        copies += [(LINE - 1 - s, LINE - 1 - a, LINE - 2 - s - i) for i, a in enumerate(parents)]
    copies.sort(key=key)
    used = [0] * LINE
    edges = []
    for s, a, b in copies:
        edges.append((s, a, b, used[a]))
        used[a] += 1
    return edges


def far_last(copy):
    s, a, b = copy
    return (abs(s - a), -abs(s - b), copy)


def outgoing(edges, s, a):
    return [e for e in edges if e[0] == s and e[1] == a]


def stops(edges):
    return sorted({(s, a) for s, a, _, _ in edges if s != a}, key=lambda c: (abs(c[0] - c[1]), c))


STEPS = len(HEADS)
FIRST = [sum(HEADS[:n]) for n in range(STEPS)]
KV_EDGES = [plan(trees, far_last) for trees in KV_TREES]
SUM_EDGES = [plan(trees, lambda copy: copy) for trees in SUM_TREES]
KV_SLOTS = 1 + max(e[3] for edges in KV_EDGES for e in edges)
SUM_SLOTS = [1 + max(e[3] for e in edges) for edges in SUM_EDGES]
PARTNERS = {frozenset((e[1], e[2])) for edges in KV_EDGES + SUM_EDGES for e in edges}


def one_of(t, members):
    found = t == members[0]
    for m in members[1:]:
        found = jnp.logical_or(found, t == m)
    return found


def kernel(nt, nh, len_hbm, route_hbm, adv_hbm, q_hbm, kv_hbm, cot_hbm, dq_hbm, dkv_hbm, *scratch):
    scratch = list(scratch)

    def take(count):
        taken = scratch[:count]
        del scratch[:count]
        return taken

    len_ref, route_ref, adv_ref, q, cot, dqb, dkvb = take(7)
    kvb, part, sums, arrived = take(STEPS), take(STEPS), take(STEPS), take(STEPS)
    g0, gsib, sel1, ga, sela, gb = [take(STEPS) for _ in range(6)]
    in_sem, own_sem, dq_sem, dkv_sem = take(4)
    kv_r, kv_s, sum_r, sum_s = take(4)
    sib_s, sib_r, a_s, a_r, b_s, b_r = take(6)

    dp = lax.axis_index("dp")
    t = lax.axis_index("tensor")
    slot = q.shape[0]
    rows = slot // nt
    kvw = nh * HEAD_DIM
    core = lax.rem(dp, 2)
    x = lax.rem(lax.div(dp, 2), 4)
    sib = dp + 1 - 2 * core
    near_a = dp + 2 * (1 - 2 * lax.rem(x, 2))
    near_b = dp + 2 * (3 - 2 * x)
    scale = 1.0 / HEAD_DIM**0.5

    barrier = pltpu.get_barrier_semaphore()

    def greet(where, index):
        pl.semaphore_signal(barrier, inc=1, device_id=(where, index), device_id_type=MESH)

    greet(sib, t)
    greet(near_a, t)
    greet(near_b, t)
    greetings = 3
    for s in range(nt):
        met = [m for m in range(nt) if frozenset((m, s)) in PARTNERS]

        @pl.when(one_of(t, met))
        def _():
            greet(dp, s)

        greetings += one_of(t, met).astype(jnp.int32)

    def remote(src, dst, send, recv, where, index):
        return pltpu.make_async_remote_copy(
            src_ref=src, dst_ref=dst, send_sem=send, recv_sem=recv, device_id=(where, index), device_id_type=MESH
        )

    def band(s):
        return pl.ds(pl.multiple_of(s * rows, rows), rows)

    def columns(n, start=0):
        return pl.ds(start + FIRST[n] * HEAD_DIM, HEADS[n] * HEAD_DIM)

    def halves(n):
        group = HEADS[n] * HEAD_DIM
        return ((columns(n), pl.ds(0, group)), (columns(n, kvw), pl.ds(group, group)))

    def own(n):
        block = kvb[n].at[band(t)]
        return pltpu.make_async_copy(block, block, own_sem.at[n])

    def kv_copy(edge, n):
        s, _, b, k = edge
        block = kvb[n].at[band(s)]
        return remote(block, block, kv_s.at[k, n], kv_r.at[s, n], dp, b)

    def kv_arrival(s, n):
        block = kvb[n].at[band(s)]
        return remote(block, block, kv_s.at[0, n], kv_r.at[s, n], dp, t)

    def sum_copy(src, edge, n):
        s, a, _, k = edge
        return remote(src[n].at[band(s)], arrived[n].at[k], sum_s.at[s, n], sum_r.at[k, n], dp, a)

    def to_sib(n):
        return remote(g0[n], gsib[n], sib_s.at[n], sib_r.at[n], sib, t)

    def to_a(n):
        return remote(sel1[n], ga[n], a_s.at[n], a_r.at[n], near_a, t)

    def to_b(n):
        return remote(sela[n], gb[n], b_s.at[n], b_r.at[n], near_b, t)

    def load_own(n):
        for there, here in halves(n):
            pltpu.make_async_copy(kv_hbm.at[:, there], kvb[n].at[band(t), here], own_sem.at[n]).start()

    def direct(n):
        own(n).wait()
        for edge in KV_EDGES[n]:
            if edge[0] == edge[1]:

                @pl.when(t == edge[1])
                def _():
                    kv_copy(edge, n).start()

    def relay(n):
        for s, a in stops(KV_EDGES[n]):

            @pl.when(t == a)
            def _():
                kv_arrival(s, n).wait_recv()
                for edge in outgoing(KV_EDGES[n], s, a):
                    kv_copy(edge, n).start()

    def arrive(n):
        for s in range(nt):
            leaves = [m for m in range(nt) if m != s and not outgoing(KV_EDGES[n], s, m)]

            @pl.when(one_of(t, leaves))
            def _():
                kv_arrival(s, n).wait_recv()

    load_cot = pltpu.make_async_copy(cot_hbm, cot, in_sem.at[0])
    load_q = pltpu.make_async_copy(q_hbm, q, in_sem.at[1])
    for n in range(STEPS):
        load_own(n)
    load_cot.start()
    small = [
        pltpu.make_async_copy(src, dst, in_sem.at[2 + i])
        for i, (src, dst) in enumerate(((len_hbm, len_ref), (route_hbm, route_ref), (adv_hbm, adv_ref)))
    ]
    for copy in small:
        copy.start()
    pl.semaphore_wait(barrier, greetings)
    for n in range(min(ISSUED, STEPS)):
        direct(n)
    load_q.start()

    for copy in small:
        copy.wait()
    code = route_ref[0]
    moved = jnp.bitwise_xor(dp, code)
    slot_len = len_ref[moved]
    factor = slot / jnp.full((1, slot), slot_len, jnp.int32).astype(jnp.float32)
    place = lax.broadcasted_iota(jnp.int32, (1, slot), 1)
    live = (place < slot_len).astype(jnp.float32)
    weight = adv_ref[...].astype(jnp.float32) / 256.0 * factor * live
    weight = jnp.broadcast_to(weight, (HEAD_DIM, slot)).T
    load_cot.wait()
    for n in range(STEPS):
        wide = jnp.concatenate([weight] * HEADS[n], axis=1)
        g0[n][...] = (cot[:, columns(n)].astype(jnp.float32) * wide).astype(jnp.bfloat16)
        to_sib(n).start()

    x_code = jnp.bitwise_and(lax.shift_right_logical(code, 1), 3)

    def chosen(n, flag):
        return jnp.full((1, HEADS[n] * HEAD_DIM), flag, jnp.int32) == 1

    use_sib = jnp.bitwise_and(code, 1)
    use_a = jnp.logical_or(x_code == 1, x_code == 2).astype(jnp.int32)
    use_b = (x_code >= 2).astype(jnp.int32)

    for n in range(STEPS):
        to_sib(n).wait_recv()
        sel1[n][...] = jnp.where(chosen(n, use_sib), gsib[n][...], g0[n][...])
        to_a(n).start()

    def hop_b(n):
        to_a(n).wait_recv()
        sela[n][...] = jnp.where(chosen(n, use_a), ga[n][...], sel1[n][...])
        to_b(n).start()

    home_len = len_ref[dp]
    key_at = lax.broadcasted_iota(jnp.int32, (slot, slot), 0)
    query_at = lax.broadcasted_iota(jnp.int32, (slot, slot), 1)

    def one_head(n, j, grad):
        here = pl.ds(j * HEAD_DIM, HEAD_DIM)
        there = pl.ds((HEADS[n] + j) * HEAD_DIM, HEAD_DIM)
        at = pl.ds((FIRST[n] + j) * HEAD_DIM, HEAD_DIM)
        query = q[:, at]
        key = kvb[n][:, here]
        value = kvb[n][:, there]
        allowed = jnp.logical_and(key_at <= query_at, key_at < home_len)
        scores = dot(key, query, NT) * scale
        dprob = dot(value, grad, NT)
        scores = jnp.where(allowed, scores, -1e30)
        expo = jnp.exp(scores - jnp.max(scores, axis=0, keepdims=True))
        probs = expo * (1.0 / jnp.sum(expo, axis=0, keepdims=True))
        probs_b = probs.astype(jnp.bfloat16)
        delta = jnp.sum(probs_b.astype(jnp.float32) * dprob, axis=0, keepdims=True)
        dscore = (probs * (dprob - delta)).astype(jnp.bfloat16)
        part[n][:, here] = (dot(dscore, query, NN) * scale).astype(jnp.bfloat16)
        part[n][:, there] = dot(probs_b, grad, NN).astype(jnp.bfloat16)
        dqb[:, at] = (dot(dscore, key, TN) * scale).astype(jnp.bfloat16)

    def compute(n):
        to_b(n).wait_recv()
        grad = jnp.where(chosen(n, use_b), gb[n][...], sela[n][...])
        for j in range(HEADS[n]):
            one_head(n, j, grad[:, j * HEAD_DIM : (j + 1) * HEAD_DIM])
        for edge in SUM_EDGES[n]:
            if not outgoing(SUM_EDGES[n], edge[0], edge[2]):

                @pl.when(t == edge[2])
                def _():
                    sum_copy(part, edge, n).start()

        store_dq(n).start()

    def store_dq(n):
        return pltpu.make_async_copy(dqb.at[:, columns(n)], dq_hbm.at[:, columns(n)], dq_sem.at[n])

    def collect(s, a, n):
        total = part[n][band(s)].astype(jnp.float32)
        for edge in outgoing(SUM_EDGES[n], s, a):
            sum_copy(sums, edge, n).wait_recv()
            total += arrived[n][edge[3]].astype(jnp.float32)
        return total.astype(jnp.bfloat16)

    def relay_sums(n):
        for s, a in sorted(stops(SUM_EDGES[n])):
            into = [e for e in SUM_EDGES[n] if e[0] == s and e[2] == a][0]

            @pl.when(t == a)
            def _():
                sums[n][band(s)] = collect(s, a, n)
                sum_copy(sums, into, n).start()

    def store_dkv(n, half):
        there = halves(n)[half][0]
        return pltpu.make_async_copy(dkvb.at[:, there], dkv_hbm.at[:, there], dkv_sem.at[n, half])

    def finish(n):
        group = HEADS[n] * HEAD_DIM
        for s in range(nt):

            @pl.when(t == s)
            def _():
                total = collect(s, s, n)
                dkvb[:, columns(n)] = total[:, 0:group]
                dkvb[:, columns(n, kvw)] = total[:, group:]

        store_dkv(n, 0).start()
        store_dkv(n, 1).start()

    def sums_sent(n):
        for edge in SUM_EDGES[n]:

            @pl.when(t == edge[2])
            def _():
                sum_copy(sums, edge, n).wait_send()

    def sent(n):
        to_sib(n).wait_send()
        to_a(n).wait_send()
        to_b(n).wait_send()
        store_dq(n).wait()
        for edge in KV_EDGES[n]:

            @pl.when(t == edge[1])
            def _():
                kv_copy(edge, n).wait_send()

    for n in range(AHEAD):
        relay(n)
    hop_b(0)
    load_q.wait()

    for n in range(STEPS + FINISH_LAG):
        if n + ISSUED < STEPS:
            direct(n + ISSUED)
        if n + AHEAD < STEPS:
            relay(n + AHEAD)
        if n + 1 < STEPS:
            hop_b(n + 1)
        if n < STEPS:
            arrive(n)
            compute(n)
        if RELAY_LAG <= n < STEPS + RELAY_LAG:
            relay_sums(n - RELAY_LAG)
        if n == STEPS + RELAY_LAG - 1:
            for m in range(STEPS):
                sent(m)
            for m in range(STEPS - 1):
                sums_sent(m)
        if n >= FINISH_LAG:
            finish(n - FINISH_LAG)

    sums_sent(STEPS - 1)
    for n in range(STEPS):
        store_dkv(n, 0).wait()
        store_dkv(n, 1).wait()


def deliver(dq_in, dkv_in, dq_out, dkv_out, dq, dkv, in_sem, out_sem):
    pieces = [(dq_in, dq, dq_out, 96, i) for i in range(dq.shape[0] // 96)]
    pieces += [(dkv_in, dkv, dkv_out, 32, i) for i in range(dkv.shape[0] // 32)]
    stages = []
    for k, (src, mid, dst, rows, i) in enumerate(pieces):
        piece = pl.ds(i * rows, rows)
        stages.append(
            (
                pltpu.make_async_copy(src.at[piece], mid.at[piece], in_sem.at[k]),
                pltpu.make_async_copy(mid.at[piece], dst.at[piece], out_sem.at[k]),
            )
        )
    for load, _ in stages:
        load.start()
    for load, store in stages:
        load.wait()
        store.start()
    for _, store in stages:
        store.wait()


def on_device(queries, keys_values, lengths, route, cotangent, advantage):
    slot, _, qwidth = queries.shape
    rows, _, kv2 = keys_values.shape
    nt = lax.axis_size("tensor")
    nh = kv2 // 2 // HEAD_DIM
    bf16 = jnp.bfloat16
    dma = pltpu.SemaphoreType.DMA
    hbm = pl.BlockSpec(memory_space=pl.ANY)
    width = [h * HEAD_DIM for h in HEADS]
    blocks = [pltpu.VMEM((slot, 2 * w), bf16) for w in width]
    grads = [pltpu.VMEM((slot, w), bf16) for w in width]
    dq, dkv = pl.pallas_call(
        functools.partial(kernel, nt, nh),
        out_shape=(
            jax.ShapeDtypeStruct((slot, qwidth), bf16),
            jax.ShapeDtypeStruct((rows, kv2), bf16),
        ),
        in_specs=[hbm] * 6,
        out_specs=(hbm, hbm),
        scratch_shapes=[
            pltpu.SMEM(lengths.shape, jnp.int32),
            pltpu.SMEM(route.shape, jnp.int32),
            pltpu.VMEM((1, slot), jnp.int32),
            pltpu.VMEM((slot, qwidth), bf16),
            pltpu.VMEM((slot, qwidth), bf16),
            pltpu.VMEM((slot, qwidth), bf16),
            pltpu.VMEM((rows, kv2), bf16),
            *blocks, *blocks, *blocks,
            *[pltpu.VMEM((k, rows, 2 * w), bf16) for k, w in zip(SUM_SLOTS, width)],
            *(grads * 6),
            dma((5,)), dma((STEPS,)), dma((STEPS,)), dma((STEPS, 2)),
            dma((nt, STEPS)), dma((KV_SLOTS, STEPS)), dma((max(SUM_SLOTS), STEPS)), dma((nt, STEPS)),
            *([dma((STEPS,))] * 6),
        ],
        compiler_params=pltpu.CompilerParams(
            collective_id=0, has_side_effects=True, vmem_limit_bytes=60 * 1024 * 1024
        ),
        name="attention_grads",
    )(
        lengths,
        route,
        advantage.reshape(1, slot),
        queries.reshape(slot, qwidth),
        keys_values.reshape(rows, kv2),
        cotangent.reshape(slot, qwidth),
    )
    dq, dkv = pl.pallas_call(
        deliver,
        out_shape=(jax.ShapeDtypeStruct(dq.shape, bf16), jax.ShapeDtypeStruct(dkv.shape, bf16)),
        in_specs=[hbm, hbm],
        out_specs=(hbm, hbm),
        scratch_shapes=[
            pltpu.VMEM(dq.shape, bf16),
            pltpu.VMEM(dkv.shape, bf16),
            dma((slot // 96 + rows // 32,)),
            dma((slot // 96 + rows // 32,)),
        ],
        compiler_params=pltpu.CompilerParams(vmem_limit_bytes=60 * 1024 * 1024),
        name="deliver",
    )(dq, dkv)
    return dq.reshape(slot, 1, qwidth), dkv.reshape(rows, 1, kv2)


def solution(mesh):
    placed = (
        P(None, "dp", "tensor"),
        P("tensor", "dp", None),
        P(),
        P(),
        P(None, "dp", "tensor"),
        P(None, "dp"),
    )
    return jax.shard_map(
        on_device,
        mesh=mesh,
        in_specs=placed,
        out_specs=(P(None, "dp", "tensor"), P("tensor", "dp", None)),
        check_vma=False,
    )
```

```python
import functools

import jax
import jax.numpy as jnp
from jax import lax
from jax.experimental import pallas as pl
from jax.experimental.pallas import tpu as pltpu
from jax.sharding import PartitionSpec as P

HEAD_DIM = 128
MESH = pl.DeviceIdType.MESH
NT = (((1,), (1,)), ((), ()))
NN = (((1,), (0,)), ((), ()))
TN = (((0,), (0,)), ((), ()))


def dot(a, b, dims):
    return lax.dot_general(a, b, dims, preferred_element_type=jnp.float32)


LINE = 6
HEADS = (2, 2, 2, 2)
AHEAD = 1
ISSUED = 4
RELAY_LAG = 2
FINISH_LAG = 4

TWO_STOPS = ((0, 1, 0, 3, 3), (1, 2, 1, 4), (2, 2, 4), (3, 4), (4,))
KV_TREES = ((TWO_STOPS, TWO_STOPS),) * len(HEADS)
SUM_TREES = ((TWO_STOPS, TWO_STOPS),) * len(HEADS)


def plan(trees, key):
    above, below = trees
    copies = []
    for s, parents in enumerate(above):
        copies += [(s, a, s + 1 + i) for i, a in enumerate(parents)]
    for s, parents in enumerate(below):
        copies += [(LINE - 1 - s, LINE - 1 - a, LINE - 2 - s - i) for i, a in enumerate(parents)]
    copies.sort(key=key)
    used = [0] * LINE
    edges = []
    for s, a, b in copies:
        edges.append((s, a, b, used[a]))
        used[a] += 1
    return edges


def far_last(copy):
    s, a, b = copy
    return (abs(s - a), -abs(s - b), copy)


def outgoing(edges, s, a):
    return [e for e in edges if e[0] == s and e[1] == a]


def stops(edges):
    return sorted({(s, a) for s, a, _, _ in edges if s != a}, key=lambda c: (abs(c[0] - c[1]), c))


STEPS = len(HEADS)
FIRST = [sum(HEADS[:n]) for n in range(STEPS)]
KV_EDGES = [plan(trees, far_last) for trees in KV_TREES]
SUM_EDGES = [plan(trees, lambda copy: copy) for trees in SUM_TREES]
KV_SLOTS = 1 + max(e[3] for edges in KV_EDGES for e in edges)
SUM_SLOTS = [1 + max(e[3] for e in edges) for edges in SUM_EDGES]
PARTNERS = {frozenset((e[1], e[2])) for edges in KV_EDGES + SUM_EDGES for e in edges}


def one_of(t, members):
    found = t == members[0]
    for m in members[1:]:
        found = jnp.logical_or(found, t == m)
    return found


def kernel(nt, nh, len_hbm, route_hbm, adv_hbm, q_hbm, kv_hbm, cot_hbm, dq_hbm, dkv_hbm, *scratch):
    scratch = list(scratch)

    def take(count):
        taken = scratch[:count]
        del scratch[:count]
        return taken

    len_ref, route_ref, adv_ref, q, cot, dqb, dkvb = take(7)
    kvb, part, sums, arrived = take(STEPS), take(STEPS), take(STEPS), take(STEPS)
    g0, gsib, sel1, ga, sela, gb = [take(STEPS) for _ in range(6)]
    in_sem, own_sem, dq_sem, dkv_sem = take(4)
    kv_r, kv_s, sum_r, sum_s = take(4)
    sib_s, sib_r, a_s, a_r, b_s, b_r = take(6)

    dp = lax.axis_index("dp")
    t = lax.axis_index("tensor")
    slot = q.shape[0]
    rows = slot // nt
    kvw = nh * HEAD_DIM
    core = lax.rem(dp, 2)
    x = lax.rem(lax.div(dp, 2), 4)
    sib = dp + 1 - 2 * core
    near_a = dp + 2 * (1 - 2 * lax.rem(x, 2))
    near_b = dp + 2 * (3 - 2 * x)
    scale = 1.0 / HEAD_DIM**0.5

    barrier = pltpu.get_barrier_semaphore()

    def greet(where, index):
        pl.semaphore_signal(barrier, inc=1, device_id=(where, index), device_id_type=MESH)

    greet(sib, t)
    greet(near_a, t)
    greet(near_b, t)
    greetings = 3
    for s in range(nt):
        met = [m for m in range(nt) if frozenset((m, s)) in PARTNERS]

        @pl.when(one_of(t, met))
        def _():
            greet(dp, s)

        greetings += one_of(t, met).astype(jnp.int32)

    def remote(src, dst, send, recv, where, index):
        return pltpu.make_async_remote_copy(
            src_ref=src, dst_ref=dst, send_sem=send, recv_sem=recv, device_id=(where, index), device_id_type=MESH
        )

    def band(s):
        return pl.ds(pl.multiple_of(s * rows, rows), rows)

    def columns(n, start=0):
        return pl.ds(start + FIRST[n] * HEAD_DIM, HEADS[n] * HEAD_DIM)

    def halves(n):
        group = HEADS[n] * HEAD_DIM
        return ((columns(n), pl.ds(0, group)), (columns(n, kvw), pl.ds(group, group)))

    def own(n):
        block = kvb[n].at[band(t)]
        return pltpu.make_async_copy(block, block, own_sem.at[n])

    def kv_copy(edge, n):
        s, _, b, k = edge
        block = kvb[n].at[band(s)]
        return remote(block, block, kv_s.at[k, n], kv_r.at[s, n], dp, b)

    def kv_arrival(s, n):
        block = kvb[n].at[band(s)]
        return remote(block, block, kv_s.at[0, n], kv_r.at[s, n], dp, t)

    def sum_copy(src, edge, n):
        s, a, _, k = edge
        return remote(src[n].at[band(s)], arrived[n].at[k], sum_s.at[s, n], sum_r.at[k, n], dp, a)

    def to_sib(n):
        return remote(g0[n], gsib[n], sib_s.at[n], sib_r.at[n], sib, t)

    def to_a(n):
        return remote(sel1[n], ga[n], a_s.at[n], a_r.at[n], near_a, t)

    def to_b(n):
        return remote(sela[n], gb[n], b_s.at[n], b_r.at[n], near_b, t)

    def load_own(n):
        for there, here in halves(n):
            pltpu.make_async_copy(kv_hbm.at[:, there], kvb[n].at[band(t), here], own_sem.at[n]).start()

    def direct(n):
        own(n).wait()
        for edge in KV_EDGES[n]:
            if edge[0] == edge[1]:

                @pl.when(t == edge[1])
                def _():
                    kv_copy(edge, n).start()

    def relay(n):
        for s, a in stops(KV_EDGES[n]):

            @pl.when(t == a)
            def _():
                kv_arrival(s, n).wait_recv()
                for edge in outgoing(KV_EDGES[n], s, a):
                    kv_copy(edge, n).start()

    def arrive(n):
        for s in range(nt):
            leaves = [m for m in range(nt) if m != s and not outgoing(KV_EDGES[n], s, m)]

            @pl.when(one_of(t, leaves))
            def _():
                kv_arrival(s, n).wait_recv()

    load_cot = pltpu.make_async_copy(cot_hbm, cot, in_sem.at[0])
    load_q = pltpu.make_async_copy(q_hbm, q, in_sem.at[1])
    for n in range(STEPS):
        load_own(n)
    load_cot.start()
    small = [
        pltpu.make_async_copy(src, dst, in_sem.at[2 + i])
        for i, (src, dst) in enumerate(((len_hbm, len_ref), (route_hbm, route_ref), (adv_hbm, adv_ref)))
    ]
    for copy in small:
        copy.start()
    pl.semaphore_wait(barrier, greetings)
    for n in range(min(ISSUED, STEPS)):
        direct(n)
    load_q.start()

    for copy in small:
        copy.wait()
    code = route_ref[0]
    moved = jnp.bitwise_xor(dp, code)
    slot_len = len_ref[moved]
    factor = slot / jnp.full((1, slot), slot_len, jnp.int32).astype(jnp.float32)
    place = lax.broadcasted_iota(jnp.int32, (1, slot), 1)
    live = (place < slot_len).astype(jnp.float32)
    weight = adv_ref[...].astype(jnp.float32) / 256.0 * factor * live
    weight = jnp.broadcast_to(weight, (HEAD_DIM, slot)).T
    load_cot.wait()
    for n in range(STEPS):
        wide = jnp.concatenate([weight] * HEADS[n], axis=1)
        g0[n][...] = (cot[:, columns(n)].astype(jnp.float32) * wide).astype(jnp.bfloat16)
        to_sib(n).start()

    x_code = jnp.bitwise_and(lax.shift_right_logical(code, 1), 3)

    def chosen(n, flag):
        return jnp.full((1, HEADS[n] * HEAD_DIM), flag, jnp.int32) == 1

    use_sib = jnp.bitwise_and(code, 1)
    use_a = jnp.logical_or(x_code == 1, x_code == 2).astype(jnp.int32)
    use_b = (x_code >= 2).astype(jnp.int32)

    for n in range(STEPS):
        to_sib(n).wait_recv()
        sel1[n][...] = jnp.where(chosen(n, use_sib), gsib[n][...], g0[n][...])
        to_a(n).start()

    def hop_b(n):
        to_a(n).wait_recv()
        sela[n][...] = jnp.where(chosen(n, use_a), ga[n][...], sel1[n][...])
        to_b(n).start()

    home_len = len_ref[dp]
    key_at = lax.broadcasted_iota(jnp.int32, (slot, slot), 0)
    query_at = lax.broadcasted_iota(jnp.int32, (slot, slot), 1)

    def one_head(n, j, grad):
        here = pl.ds(j * HEAD_DIM, HEAD_DIM)
        there = pl.ds((HEADS[n] + j) * HEAD_DIM, HEAD_DIM)
        at = pl.ds((FIRST[n] + j) * HEAD_DIM, HEAD_DIM)
        query = q[:, at]
        key = kvb[n][:, here]
        value = kvb[n][:, there]
        allowed = jnp.logical_and(key_at <= query_at, key_at < home_len)
        scores = dot(key, query, NT) * scale
        dprob = dot(value, grad, NT)
        scores = jnp.where(allowed, scores, -1e30)
        expo = jnp.exp(scores - jnp.max(scores, axis=0, keepdims=True))
        probs = expo * (1.0 / jnp.sum(expo, axis=0, keepdims=True))
        probs_b = probs.astype(jnp.bfloat16)
        delta = jnp.sum(probs_b.astype(jnp.float32) * dprob, axis=0, keepdims=True)
        dscore = (probs * (dprob - delta)).astype(jnp.bfloat16)
        part[n][:, here] = (dot(dscore, query, NN) * scale).astype(jnp.bfloat16)
        part[n][:, there] = dot(probs_b, grad, NN).astype(jnp.bfloat16)
        dqb[:, at] = (dot(dscore, key, TN) * scale).astype(jnp.bfloat16)

    def compute(n):
        to_b(n).wait_recv()
        grad = jnp.where(chosen(n, use_b), gb[n][...], sela[n][...])
        for j in range(HEADS[n]):
            one_head(n, j, grad[:, j * HEAD_DIM : (j + 1) * HEAD_DIM])
        for edge in SUM_EDGES[n]:
            if not outgoing(SUM_EDGES[n], edge[0], edge[2]):

                @pl.when(t == edge[2])
                def _():
                    sum_copy(part, edge, n).start()

        store_dq(n).start()

    def store_dq(n):
        return pltpu.make_async_copy(dqb.at[:, columns(n)], dq_hbm.at[:, columns(n)], dq_sem.at[n])

    def collect(s, a, n):
        total = part[n][band(s)].astype(jnp.float32)
        for edge in outgoing(SUM_EDGES[n], s, a):
            sum_copy(sums, edge, n).wait_recv()
            total += arrived[n][edge[3]].astype(jnp.float32)
        return total.astype(jnp.bfloat16)

    def relay_sums(n):
        for s, a in sorted(stops(SUM_EDGES[n])):
            into = [e for e in SUM_EDGES[n] if e[0] == s and e[2] == a][0]

            @pl.when(t == a)
            def _():
                sums[n][band(s)] = collect(s, a, n)
                sum_copy(sums, into, n).start()

    def store_dkv(n, half):
        there = halves(n)[half][0]
        return pltpu.make_async_copy(dkvb.at[:, there], dkv_hbm.at[:, there], dkv_sem.at[n, half])

    def finish(n):
        group = HEADS[n] * HEAD_DIM
        for s in range(nt):

            @pl.when(t == s)
            def _():
                total = collect(s, s, n)
                dkvb[:, columns(n)] = total[:, 0:group]
                dkvb[:, columns(n, kvw)] = total[:, group:]

        store_dkv(n, 0).start()
        store_dkv(n, 1).start()

    def sums_sent(n):
        for edge in SUM_EDGES[n]:

            @pl.when(t == edge[2])
            def _():
                sum_copy(sums, edge, n).wait_send()

    def sent(n):
        to_sib(n).wait_send()
        to_a(n).wait_send()
        to_b(n).wait_send()
        store_dq(n).wait()
        for edge in KV_EDGES[n]:

            @pl.when(t == edge[1])
            def _():
                kv_copy(edge, n).wait_send()

    hop_b(0)
    for n in range(AHEAD):
        relay(n)
    hop_b(1)
    load_q.wait()

    for n in range(STEPS + FINISH_LAG):
        if n + ISSUED < STEPS:
            direct(n + ISSUED)
        if n + AHEAD < STEPS:
            relay(n + AHEAD)
        if n + 2 < STEPS:
            hop_b(n + 2)
        if n < STEPS:
            arrive(n)
            compute(n)
        if RELAY_LAG <= n < STEPS + RELAY_LAG:
            relay_sums(n - RELAY_LAG)
        if n == STEPS + RELAY_LAG - 1:
            for m in range(STEPS):
                sent(m)
            for m in range(STEPS - 1):
                sums_sent(m)
        if n >= FINISH_LAG:
            finish(n - FINISH_LAG)

    sums_sent(STEPS - 1)
    for n in range(STEPS):
        store_dkv(n, 0).wait()
        store_dkv(n, 1).wait()


def deliver(dq_in, dkv_in, dq_out, dkv_out, dq, dkv, in_sem, out_sem):
    pieces = [(dq_in, dq, dq_out, 96, i) for i in range(dq.shape[0] // 96)]
    pieces += [(dkv_in, dkv, dkv_out, 32, i) for i in range(dkv.shape[0] // 32)]
    stages = []
    for k, (src, mid, dst, rows, i) in enumerate(pieces):
        piece = pl.ds(i * rows, rows)
        stages.append(
            (
                pltpu.make_async_copy(src.at[piece], mid.at[piece], in_sem.at[k]),
                pltpu.make_async_copy(mid.at[piece], dst.at[piece], out_sem.at[k]),
            )
        )
    for load, _ in stages:
        load.start()
    for load, store in stages:
        load.wait()
        store.start()
    for _, store in stages:
        store.wait()


def on_device(queries, keys_values, lengths, route, cotangent, advantage):
    slot, _, qwidth = queries.shape
    rows, _, kv2 = keys_values.shape
    nt = lax.axis_size("tensor")
    nh = kv2 // 2 // HEAD_DIM
    bf16 = jnp.bfloat16
    dma = pltpu.SemaphoreType.DMA
    hbm = pl.BlockSpec(memory_space=pl.ANY)
    width = [h * HEAD_DIM for h in HEADS]
    blocks = [pltpu.VMEM((slot, 2 * w), bf16) for w in width]
    grads = [pltpu.VMEM((slot, w), bf16) for w in width]
    dq, dkv = pl.pallas_call(
        functools.partial(kernel, nt, nh),
        out_shape=(
            jax.ShapeDtypeStruct((slot, qwidth), bf16),
            jax.ShapeDtypeStruct((rows, kv2), bf16),
        ),
        in_specs=[hbm] * 6,
        out_specs=(hbm, hbm),
        scratch_shapes=[
            pltpu.SMEM(lengths.shape, jnp.int32),
            pltpu.SMEM(route.shape, jnp.int32),
            pltpu.VMEM((1, slot), jnp.int32),
            pltpu.VMEM((slot, qwidth), bf16),
            pltpu.VMEM((slot, qwidth), bf16),
            pltpu.VMEM((slot, qwidth), bf16),
            pltpu.VMEM((rows, kv2), bf16),
            *blocks, *blocks, *blocks,
            *[pltpu.VMEM((k, rows, 2 * w), bf16) for k, w in zip(SUM_SLOTS, width)],
            *(grads * 6),
            dma((5,)), dma((STEPS,)), dma((STEPS,)), dma((STEPS, 2)),
            dma((nt, STEPS)), dma((KV_SLOTS, STEPS)), dma((max(SUM_SLOTS), STEPS)), dma((nt, STEPS)),
            *([dma((STEPS,))] * 6),
        ],
        compiler_params=pltpu.CompilerParams(
            collective_id=0, has_side_effects=True, vmem_limit_bytes=60 * 1024 * 1024
        ),
        name="attention_grads",
    )(
        lengths,
        route,
        advantage.reshape(1, slot),
        queries.reshape(slot, qwidth),
        keys_values.reshape(rows, kv2),
        cotangent.reshape(slot, qwidth),
    )
    dq, dkv = pl.pallas_call(
        deliver,
        out_shape=(jax.ShapeDtypeStruct(dq.shape, bf16), jax.ShapeDtypeStruct(dkv.shape, bf16)),
        in_specs=[hbm, hbm],
        out_specs=(hbm, hbm),
        scratch_shapes=[
            pltpu.VMEM(dq.shape, bf16),
            pltpu.VMEM(dkv.shape, bf16),
            dma((slot // 96 + rows // 32,)),
            dma((slot // 96 + rows // 32,)),
        ],
        compiler_params=pltpu.CompilerParams(vmem_limit_bytes=60 * 1024 * 1024),
        name="deliver",
    )(dq, dkv)
    return dq.reshape(slot, 1, qwidth), dkv.reshape(rows, 1, kv2)


def solution(mesh):
    placed = (
        P(None, "dp", "tensor"),
        P("tensor", "dp", None),
        P(),
        P(),
        P(None, "dp", "tensor"),
        P(None, "dp"),
    )
    return jax.shard_map(
        on_device,
        mesh=mesh,
        in_specs=placed,
        out_specs=(P(None, "dp", "tensor"), P("tensor", "dp", None)),
        check_vma=False,
    )
```
